32 devices in a mesh: tm: 16 (over z, y, x), chan: 2 (over core).
Axes of the slice: x: 2, y: 2, z: 4, core: 2. Of those that a mesh axis runs over, the one named last changes fastest.
Arguments:
- frames: bfloat16 [128, 16, 16, 256], P('tm'), may hold values from -6 to 6
- in_weight: bfloat16 [3, 3, 256, 1024], P(None, None, None, 'chan'), may hold values from -0.125 to 0.125
- decay_codes: int32 [1024], P('chan'), may hold values from 1 to 20
- out_weight: bfloat16 [3, 3, 1024, 256], P(None, None, 'chan'), may hold values from -0.00390625 to 0.00390625
- skip_gain: float32 [256], replicated, may hold values from 0.5 to 1.5
Outputs:
- mixed: bfloat16 [128, 16, 16, 256], P('tm', 'chan')
The draws below stay inside these ranges and needn't reach their ends.
Inputs may be any that keep to these rules, and one draw needn't show every extreme that they name: `decay_codes`: a code k gives the channel the decay 1 - k / 4096.
All inputs are finite; a program needn't handle non-finite values.
Results may differ from the reference program's by a relative error of at most 0.0037.
Values sent between devices are 32-bit elements; how exact they have to be, the bound alone decides.
A program may use at most 64 MiB of HBM per device.

```python
import jax
import jax.numpy as jnp
from jax import lax

CIN = 256
P_SIZE = 1024
H = 16
W = 16
TT = 128


def with_ends(entries, rng, smallest, top_value):
    dims = entries.shape
    place = [jax.random.randint(jax.random.fold_in(rng, axis), (), 0, dims[axis]) for axis in range(len(dims))]
    entries = entries.at[tuple(place)].set(smallest)
    longest = dims.index(max(dims))
    place[longest] = (place[longest] + 1) % dims[longest]
    return entries.at[tuple(place)].set(top_value)


def shard_levels(own_key, dims, pieces, low, high):
    factor_of = 1.0
    for position, shards_of in pieces:
        draws = jax.random.uniform(jax.random.fold_in(jax.random.fold_in(own_key, 6), position), (shards_of,), jnp.float32, low / len(pieces), high / len(pieces))
        factor_of = factor_of * jnp.repeat(jnp.exp(draws), dims[position] // shards_of).reshape((-1,) + (1,) * (len(dims) - 1 - position))
    return factor_of


def normal_values(rng, extent, scale, limit, shards=(), dtype=jnp.bfloat16):
    drawn = scale * jax.random.normal(rng, extent, jnp.float32)
    if shards:
        drawn = drawn * shard_levels(rng, extent, shards, -0.22, 0.18)
    return jnp.clip(drawn, -limit, limit).astype(dtype)


def setup_inputs(seed: int = 0) -> dict:
    arg_keys = jax.random.split(jax.random.key(seed), 6)
    return {
        "frames": normal_values(arg_keys[0], (TT, H, W, CIN), 1.0, 6.0, ((0, 16),)),
        "in_weight": normal_values(arg_keys[1], (3, 3, CIN, P_SIZE), (9 * CIN) ** -0.5, 0.125, ((3, 2),)),
        "decay_codes": with_ends(jax.random.randint(arg_keys[2], (P_SIZE,), 1, 21), jax.random.fold_in(arg_keys[2], 1), 1, 20).astype(jnp.int32),
        "out_weight": normal_values(arg_keys[3], (3, 3, P_SIZE, CIN), (9 * P_SIZE * 256) ** -0.5, 0.00390625, ((2, 2),)),
        "skip_gain": jnp.clip(jax.random.uniform(arg_keys[4], (CIN,), jnp.float32, 0.5, 1.5), 0.5, 1.5),
    }


def convolve(inputs, kernel):
    return lax.conv_general_dilated(inputs, kernel, (1, 1), "SAME", dimension_numbers=("NHWC", "HWIO", "NHWC"), preferred_element_type=jnp.float32)


def reference(frames, in_weight, decay_codes, out_weight, skip_gain):
    drive_term = convolve(frames, in_weight)
    decay_rate = 1.0 - decay_codes.astype(jnp.float32) / 4096.0

    def advance_step(carry_state, drive_frame):
        carry_state = decay_rate * carry_state + drive_frame
        return carry_state, carry_state

    final_state, states = lax.scan(advance_step, jnp.zeros(drive_term.shape[1:], jnp.float32), drive_term)
    state_b = states.astype(jnp.bfloat16)
    combined = convolve(state_b, out_weight) + skip_gain * frames.astype(jnp.float32)
    return jax.nn.gelu(combined, approximate=False).astype(jnp.bfloat16)
```

```python
import functools

import jax
import jax.numpy as jnp
from jax import lax
from jax.experimental import pallas as pl
from jax.experimental.pallas import tpu as pltpu
from jax.sharding import PartitionSpec as P

MESH = pl.DeviceIdType.MESH


def factor(count, rows):
    low = 1
    while low * low < count or count % low or rows % low:
        low += 1
    return count // low, low


def shifted(value, width):
    n = value.shape[0]
    column = lax.rem(lax.broadcasted_iota(jnp.int32, value.shape, 0), width)
    left = jnp.where(column == 0, 0.0, pltpu.roll(value, 1, 0))
    right = jnp.where(column == width - 1, 0.0, pltpu.roll(value, n - 1, 0))
    return left, value, right


def kernel(n_tm, n_chan, frames_ref, win_ref, codes_ref, wout_ref, out_ref,
           fpad, spad, loc, recv_a, pre, total, recv_b, carry, part, recv_d,
           a_send, a_recv, b_send, b_recv, c_send, c_recv, d_send, d_recv):
    frame_count, height, width, cin = frames_ref.shape
    p = win_ref.shape[-1]
    hi, lo = factor(n_tm, height)
    block = height // lo
    own_rows = height // n_chan
    me = lax.axis_index("tm")
    chan = lax.axis_index("chan")
    high, low = me // lo, lax.rem(me, lo)

    def mate(k):
        return lax.rem(low + k, lo)

    def at_tm(index):
        return {"tm": index, "chan": chan}

    def at_chan(index):
        return {"tm": me, "chan": index}

    barrier = pltpu.get_barrier_semaphore()
    for k in range(1, lo):
        pl.semaphore_signal(barrier, inc=1, device_id=at_tm(high * lo + mate(k)), device_id_type=MESH)
    for k in range(1, n_chan):
        pl.semaphore_signal(barrier, inc=1, device_id=at_chan(lax.rem(chan + k, n_chan)), device_id_type=MESH)

    @pl.when(high > 0)
    def _():
        pl.semaphore_signal(barrier, inc=1, device_id=at_tm(me - lo), device_id_type=MESH)

    @pl.when(high < hi - 1)
    def _():
        pl.semaphore_signal(barrier, inc=1, device_id=at_tm(me + lo), device_id_type=MESH)

    fpad[:, 0] = jnp.zeros((frame_count, width, 3 * cin), jnp.bfloat16)
    fpad[:, height + 1] = jnp.zeros((frame_count, width, 3 * cin), jnp.bfloat16)
    spad[:, 0] = jnp.zeros((frame_count, width, 3 * p), jnp.bfloat16)
    spad[:, height + 1] = jnp.zeros((frame_count, width, 3 * p), jnp.bfloat16)

    @pl.loop(0, frame_count)
    def _(f):
        value = frames_ref[f].astype(jnp.float32).reshape(height * width, cin)
        for dj, piece in enumerate(shifted(value, width)):
            fpad[f, 1 : height + 1, :, dj * cin : (dj + 1) * cin] = piece.astype(jnp.bfloat16).reshape(height, width, cin)

    decay = 1.0 - codes_ref[...].astype(jnp.float32) / 4096.0
    powers = [decay]
    for _ in range(1, frame_count):
        powers.append(powers[-1] * decay)
    step = powers[-1]
    steps = [jnp.ones_like(step)]
    for _ in range(lo):
        steps.append(steps[-1] * step)

    peers = lo + n_chan - 2 + jnp.where(high > 0, 1, 0) + jnp.where(high < hi - 1, 1, 0)
    pl.semaphore_wait(barrier, peers)

    def copy_a(k):
        return pltpu.make_async_remote_copy(
            src_ref=loc.at[frame_count - 1, pl.ds(mate(k) * block, block)],
            dst_ref=recv_a.at[low],
            send_sem=a_send.at[k], recv_sem=a_recv.at[k],
            device_id=at_tm(high * lo + mate(k)), device_id_type=MESH)

    for k in list(range(1, lo)) + [0]:
        first = mate(k) * block
        drive = None
        for di in range(3):
            lhs = fpad[:, pl.ds(first + di, block)].reshape(frame_count * block * width, 3 * cin)
            term = jnp.dot(lhs, win_ref[di], preferred_element_type=jnp.float32)
            drive = term if drive is None else drive + term
        drive = drive.reshape(frame_count, block * width, p)
        running = drive[0]
        loc[0, pl.ds(first, block)] = running.reshape(block, width, p)
        for f in range(1, frame_count):
            running = decay * running + drive[f]
            loc[f, pl.ds(first, block)] = running.reshape(block, width, p)
        if k:
            copy_a(k).start()
        else:
            recv_a[low] = running.reshape(block, width, p)

    for k in range(1, lo):
        copy_a(k).wait_recv()

    def copy_b(row):
        return pltpu.make_async_remote_copy(
            src_ref=total.at[row], dst_ref=recv_b.at[row],
            send_sem=b_send.at[row], recv_sem=b_recv.at[row],
            device_id=at_tm(lax.rem(me + lo, n_tm)), device_id_type=MESH)

    def copy_c(k, row):
        return pltpu.make_async_remote_copy(
            src_ref=pre.at[mate(k), row], dst_ref=carry.at[low * block + row],
            send_sem=c_send.at[k, row], recv_sem=c_recv.at[k, row],
            device_id=at_tm(high * lo + mate(k)), device_id_type=MESH)

    for row in range(block):
        running = jnp.zeros((width, p), jnp.float32)
        for i in range(lo):
            pre[i, row] = running
            running = step * running + recv_a[i, row]
        total[row] = running

    for row in range(block):
        @pl.when(high == 0)
        def _():
            recv_b[row] = jnp.zeros((width, p), jnp.float32)

        @pl.when(high > 0)
        def _():
            copy_b(row).wait_recv()

        entering = recv_b[row]

        @pl.when(high < hi - 1)
        def _():
            total[row] = steps[lo] * entering + total[row]
            copy_b(row).start()

        for i in range(lo):
            pre[i, row] = pre[i, row] + steps[i] * entering
        for k in range(1, lo):
            copy_c(k, row).start()
        carry[low * block + row] = pre[low, row]

    for k in range(lo):
        source = lax.rem(low + lo - k, lo)
        if k:
            for row in range(block):
                copy_c(k, row).wait_recv()
        first = source * block
        entering = carry[pl.ds(first, block)].reshape(block * width, p)
        for f in range(frame_count):
            value = loc[f, pl.ds(first, block)].reshape(block * width, p) + powers[f] * entering
            for dj, piece in enumerate(shifted(value, width)):
                spad[f, pl.ds(first + 1, block), :, dj * p : (dj + 1) * p] = piece.astype(jnp.bfloat16).reshape(block, width, p)

    def copy_d(k):
        return pltpu.make_async_remote_copy(
            src_ref=part.at[k], dst_ref=recv_d.at[k],
            send_sem=d_send.at[k], recv_sem=d_recv.at[k],
            device_id=at_chan(lax.rem(chan + k, n_chan)), device_id_type=MESH)

    piece_rows = min(own_rows, 4)
    for k in list(range(1, n_chan)) + [0]:
        for start in range(0, own_rows, piece_rows):
            first = lax.rem(chan + k, n_chan) * own_rows + start
            readout = None
            for di in range(3):
                lhs = spad[:, pl.ds(first + di, piece_rows)].reshape(frame_count * piece_rows * width, 3 * p)
                term = jnp.dot(lhs, wout_ref[di], preferred_element_type=jnp.float32)
                readout = term if readout is None else readout + term
            part[k, :, start : start + piece_rows] = readout.reshape(frame_count, piece_rows, width, cin)
        if k:
            copy_d(k).start()

    for k in range(1, n_chan):
        copy_d(k).wait_recv()
    for f in range(frame_count):
        value = part[0, f]
        for k in range(1, n_chan):
            value = value + recv_d[k, f]
        out_ref[f] = value

    for k in range(1, n_chan):
        copy_d(k).wait_send()
    for k in range(1, lo):
        copy_a(k).wait_send()
        for row in range(block):
            copy_c(k, row).wait_send()
    for row in range(block):
        @pl.when(high < hi - 1)
        def _():
            copy_b(row).wait_send()


def per_device(n_tm, n_chan, frames, in_weight, decay_codes, out_weight, skip_gain):
    frame_count, height, width, cin = frames.shape
    p = in_weight.shape[-1]
    hi, lo = factor(n_tm, height)
    block = height // lo
    own_rows = height // n_chan
    f32, bf16 = jnp.float32, jnp.bfloat16
    dma = pltpu.SemaphoreType.DMA
    summed = pl.pallas_call(
        functools.partial(kernel, n_tm, n_chan),
        out_shape=jax.ShapeDtypeStruct((frame_count, own_rows, width, cin), f32),
        in_specs=[pl.BlockSpec(memory_space=pltpu.VMEM)] * 4,
        out_specs=pl.BlockSpec(memory_space=pltpu.VMEM),
        scratch_shapes=[
            pltpu.VMEM((frame_count, height + 2, width, 3 * cin), bf16),
            pltpu.VMEM((frame_count, height + 2, width, 3 * p), bf16),
            pltpu.VMEM((frame_count, height, width, p), f32),
            pltpu.VMEM((lo, block, width, p), f32),
            pltpu.VMEM((lo, block, width, p), f32),
            pltpu.VMEM((block, width, p), f32),
            pltpu.VMEM((block, width, p), f32),
            pltpu.VMEM((height, width, p), f32),
            pltpu.VMEM((n_chan, frame_count, own_rows, width, cin), f32),
            pltpu.VMEM((n_chan, frame_count, own_rows, width, cin), f32),
            dma((lo,)), dma((lo,)), dma((block,)), dma((block,)),
            dma((lo, block)), dma((lo, block)), dma((n_chan,)), dma((n_chan,)),
        ],
        compiler_params=pltpu.CompilerParams(
            collective_id=0, has_side_effects=True, vmem_limit_bytes=56 * 1024 * 1024),
    )(
        frames,
        in_weight.reshape(3, 3 * cin, p),
        decay_codes.reshape(1, p),
        out_weight.reshape(3, 3 * p, cin),
    )
    start_row = lax.axis_index("chan") * own_rows
    own_frames = lax.dynamic_slice_in_dim(frames, start_row, own_rows, 1).astype(f32)
    return jax.nn.gelu(summed + skip_gain * own_frames, approximate=False).astype(bf16)


def solution(mesh):
    return jax.shard_map(
        functools.partial(per_device, mesh.shape["tm"], mesh.shape["chan"]),
        mesh=mesh,
        in_specs=(
            P("tm", None, None, None),
            P(None, None, None, "chan"),
            P("chan"),
            P(None, None, "chan", None),
            P(),
        ),
        out_specs=P("tm", "chan", None, None),
        check_vma=False,
    )
```

```python
import functools

import jax
import jax.numpy as jnp
from jax import lax
from jax.experimental import pallas as pl
from jax.experimental.pallas import tpu as pltpu
from jax.sharding import PartitionSpec as P

MESH = pl.DeviceIdType.MESH


def factor(count, rows):
    low = 1
    while low * low < count or count % low or rows % low:
        low += 1
    return count // low, low


def shifted(value, width):
    n = value.shape[0]
    column = lax.rem(lax.broadcasted_iota(jnp.int32, value.shape, 0), width)
    left = jnp.where(column == 0, 0.0, pltpu.roll(value, 1, 0))
    right = jnp.where(column == width - 1, 0.0, pltpu.roll(value, n - 1, 0))
    return left, value, right


def kernel(n_tm, n_chan, frames_ref, win_ref, codes_ref, wout_ref, out_ref,
           fpad, spad, loc, recv_a, pre, total, recv_b, carry, part, recv_d, win, wout,
           w_sem, a_send, a_recv, b_send, b_recv, c_send, c_recv, d_send, d_recv):
    frame_count, height, width, cin = frames_ref.shape
    p = win_ref.shape[-1]
    groups = loc.shape[0]
    pg = p // groups
    hi, lo = factor(n_tm, height)
    block = height // lo
    own_rows = height // n_chan
    me = lax.axis_index("tm")
    chan = lax.axis_index("chan")
    high, low = me // lo, lax.rem(me, lo)

    def mate(k):
        return lax.rem(low + k, lo)

    def at_tm(index):
        return {"tm": index, "chan": chan}

    def at_chan(index):
        return {"tm": me, "chan": index}

    load_in = pltpu.make_async_copy(win_ref, win, w_sem.at[0])
    load_out = pltpu.make_async_copy(wout_ref, wout, w_sem.at[1])
    load_in.start()
    load_out.start()

    barrier = pltpu.get_barrier_semaphore()
    for k in range(1, lo):
        pl.semaphore_signal(barrier, inc=1, device_id=at_tm(high * lo + mate(k)), device_id_type=MESH)
    for k in range(1, n_chan):
        pl.semaphore_signal(barrier, inc=1, device_id=at_chan(lax.rem(chan + k, n_chan)), device_id_type=MESH)

    @pl.when(high > 0)
    def _():
        pl.semaphore_signal(barrier, inc=1, device_id=at_tm(me - lo), device_id_type=MESH)

    @pl.when(high < hi - 1)
    def _():
        pl.semaphore_signal(barrier, inc=1, device_id=at_tm(me + lo), device_id_type=MESH)

    fpad[:, 0] = jnp.zeros((frame_count, width, 3 * cin), jnp.bfloat16)
    fpad[:, height + 1] = jnp.zeros((frame_count, width, 3 * cin), jnp.bfloat16)
    spad[:, 0] = jnp.zeros((frame_count, width, 3 * p), jnp.bfloat16)
    spad[:, height + 1] = jnp.zeros((frame_count, width, 3 * p), jnp.bfloat16)

    @pl.loop(0, frame_count)
    def _(f):
        value = frames_ref[f].astype(jnp.float32).reshape(height * width, cin)
        for dj, piece in enumerate(shifted(value, width)):
            fpad[f, 1 : height + 1, :, dj * cin : (dj + 1) * cin] = piece.astype(jnp.bfloat16).reshape(height, width, cin)

    decay = 1.0 - codes_ref[...].astype(jnp.float32) / 4096.0
    powers = [decay]
    for _ in range(1, frame_count):
        powers.append(powers[-1] * decay)
    step = powers[-1]
    steps = [jnp.ones_like(step)]
    for _ in range(lo):
        steps.append(steps[-1] * step)

    peers = lo + n_chan - 2 + jnp.where(high > 0, 1, 0) + jnp.where(high < hi - 1, 1, 0)
    pl.semaphore_wait(barrier, peers)

    def lanes(vectors, g):
        return [vector[:, g * pg : (g + 1) * pg] for vector in vectors]

    def copy_a(g, k):
        return pltpu.make_async_remote_copy(
            src_ref=loc.at[g, frame_count - 1, pl.ds(mate(k) * block, block)],
            dst_ref=recv_a.at[g, low],
            send_sem=a_send.at[g, k], recv_sem=a_recv.at[g, k],
            device_id=at_tm(high * lo + mate(k)), device_id_type=MESH)

    def copy_b(g, row):
        return pltpu.make_async_remote_copy(
            src_ref=total.at[g, row], dst_ref=recv_b.at[g, row],
            send_sem=b_send.at[g, row], recv_sem=b_recv.at[g, row],
            device_id=at_tm(lax.rem(me + lo, n_tm)), device_id_type=MESH)

    def copy_c(g, k, row):
        return pltpu.make_async_remote_copy(
            src_ref=pre.at[g, mate(k), row], dst_ref=carry.at[g, low * block + row],
            send_sem=c_send.at[g, k, row], recv_sem=c_recv.at[g, k, row],
            device_id=at_tm(high * lo + mate(k)), device_id_type=MESH)

    load_in.wait()
    for g in range(groups):
        (rate,) = lanes([decay], g)
        for k in list(range(1, lo)) + [0]:
            first = mate(k) * block
            drive = None
            for di in range(3):
                lhs = fpad[:, pl.ds(first + di, block)].reshape(frame_count * block * width, 3 * cin)
                term = jnp.dot(lhs, win[di, :, g * pg : (g + 1) * pg], preferred_element_type=jnp.float32)
                drive = term if drive is None else drive + term
            drive = drive.reshape(frame_count, block * width, pg)
            running = drive[0]
            loc[g, 0, pl.ds(first, block)] = running.reshape(block, width, pg)
            for f in range(1, frame_count):
                running = rate * running + drive[f]
                loc[g, f, pl.ds(first, block)] = running.reshape(block, width, pg)
            if k:
                copy_a(g, k).start()
            else:
                recv_a[g, low] = running.reshape(block, width, pg)

    for g in range(groups):
        jumps = lanes(steps, g)
        for k in range(1, lo):
            copy_a(g, k).wait_recv()
        for row in range(block):
            running = jnp.zeros((width, pg), jnp.float32)
            for i in range(lo):
                pre[g, i, row] = running
                running = jumps[1] * running + recv_a[g, i, row]
            total[g, row] = running
        for row in range(block):
            @pl.when(high == 0)
            def _():
                recv_b[g, row] = jnp.zeros((width, pg), jnp.float32)

            @pl.when(high > 0)
            def _():
                copy_b(g, row).wait_recv()

            entering = recv_b[g, row]

            @pl.when(high < hi - 1)
            def _():
                total[g, row] = jumps[lo] * entering + total[g, row]
                copy_b(g, row).start()

            for i in range(lo):
                pre[g, i, row] = pre[g, i, row] + jumps[i] * entering
            for k in range(1, lo):
                copy_c(g, k, row).start()
            carry[g, low * block + row] = pre[g, low, row]

    def copy_d(k):
        return pltpu.make_async_remote_copy(
            src_ref=part.at[k], dst_ref=recv_d.at[k],
            send_sem=d_send.at[k], recv_sem=d_recv.at[k],
            device_id=at_chan(lax.rem(chan + k, n_chan)), device_id_type=MESH)

    load_out.wait()
    piece_rows = min(own_rows, 4)
    for g in range(groups):
        rates = lanes(powers, g)
        for k in range(lo):
            source = lax.rem(low + lo - k, lo)
            if k:
                for row in range(block):
                    copy_c(g, k, row).wait_recv()
            first = source * block
            entering = carry[g, pl.ds(first, block)].reshape(block * width, pg)
            for f in range(frame_count):
                value = loc[g, f, pl.ds(first, block)].reshape(block * width, pg) + rates[f] * entering
                for dj, piece in enumerate(shifted(value, width)):
                    at = (3 * g + dj) * pg
                    spad[f, pl.ds(first + 1, block), :, at : at + pg] = piece.astype(jnp.bfloat16).reshape(block, width, pg)
        for k in list(range(1, n_chan)) + [0]:
            for start in range(0, own_rows, piece_rows):
                first = lax.rem(chan + k, n_chan) * own_rows + start
                readout = None
                for di in range(3):
                    lhs = spad[:, pl.ds(first + di, piece_rows), :, 3 * g * pg : 3 * (g + 1) * pg]
                    lhs = lhs.reshape(frame_count * piece_rows * width, 3 * pg)
                    rhs = jnp.concatenate([wout[di, dj, g * pg : (g + 1) * pg] for dj in range(3)], axis=0)
                    term = jnp.dot(lhs, rhs, preferred_element_type=jnp.float32)
                    readout = term if readout is None else readout + term
                readout = readout.reshape(frame_count, piece_rows, width, cin)
                if g:
                    readout = readout + part[k, :, start : start + piece_rows]
                part[k, :, start : start + piece_rows] = readout
            if k and g == groups - 1:
                copy_d(k).start()

    for k in range(1, n_chan):
        copy_d(k).wait_recv()
    for f in range(frame_count):
        value = part[0, f]
        for k in range(1, n_chan):
            value = value + recv_d[k, f]
        out_ref[f] = value

    for k in range(1, n_chan):
        copy_d(k).wait_send()
    for g in range(groups):
        for k in range(1, lo):
            copy_a(g, k).wait_send()
            for row in range(block):
                copy_c(g, k, row).wait_send()
        for row in range(block):
            @pl.when(high < hi - 1)
            def _():
                copy_b(g, row).wait_send()


def per_device(n_tm, n_chan, frames, in_weight, decay_codes, out_weight, skip_gain):
    frame_count, height, width, cin = frames.shape
    p = in_weight.shape[-1]
    hi, lo = factor(n_tm, height)
    block = height // lo
    own_rows = height // n_chan
    groups = 2 if p % 512 == 0 else 1
    pg = p // groups
    f32, bf16 = jnp.float32, jnp.bfloat16
    dma = pltpu.SemaphoreType.DMA
    summed = pl.pallas_call(
        functools.partial(kernel, n_tm, n_chan),
        out_shape=jax.ShapeDtypeStruct((frame_count, own_rows, width, cin), f32),
        in_specs=[
            pl.BlockSpec(memory_space=pltpu.VMEM),
            pl.BlockSpec(memory_space=pl.ANY),
            pl.BlockSpec(memory_space=pltpu.VMEM),
            pl.BlockSpec(memory_space=pl.ANY),
        ],
        out_specs=pl.BlockSpec(memory_space=pltpu.VMEM),
        scratch_shapes=[
            pltpu.VMEM((frame_count, height + 2, width, 3 * cin), bf16),
            pltpu.VMEM((frame_count, height + 2, width, 3 * p), bf16),
            pltpu.VMEM((groups, frame_count, height, width, pg), f32),
            pltpu.VMEM((groups, lo, block, width, pg), f32),
            pltpu.VMEM((groups, lo, block, width, pg), f32),
            pltpu.VMEM((groups, block, width, pg), f32),
            pltpu.VMEM((groups, block, width, pg), f32),
            pltpu.VMEM((groups, height, width, pg), f32),
            pltpu.VMEM((n_chan, frame_count, own_rows, width, cin), f32),
            pltpu.VMEM((n_chan, frame_count, own_rows, width, cin), f32),
            pltpu.VMEM((3, 3 * cin, p), bf16),
            pltpu.VMEM((3, 3, p, cin), bf16),
            dma((2,)), dma((groups, lo)), dma((groups, lo)), dma((groups, block)), dma((groups, block)),
            dma((groups, lo, block)), dma((groups, lo, block)), dma((n_chan,)), dma((n_chan,)),
        ],
        compiler_params=pltpu.CompilerParams(
            collective_id=0, has_side_effects=True, vmem_limit_bytes=56 * 1024 * 1024),
    )(
        frames,
        in_weight.reshape(3, 3 * cin, p),
        decay_codes.reshape(1, p),
        out_weight,
    )
    start_row = lax.axis_index("chan") * own_rows
    own_frames = lax.dynamic_slice_in_dim(frames, start_row, own_rows, 1).astype(f32)
    value = summed + skip_gain * own_frames
    return (0.5 * value * (1.0 + lax.erf(value * 0.5**0.5))).astype(bf16)


def solution(mesh):
    return jax.shard_map(
        functools.partial(per_device, mesh.shape["tm"], mesh.shape["chan"]),
        mesh=mesh,
        in_specs=(
            P("tm", None, None, None),
            P(None, None, None, "chan"),
            P("chan"),
            P(None, None, "chan", None),
            P(),
        ),
        out_specs=P("tm", "chan", None, None),
        check_vma=False,
    )
```

```python
import functools

import jax
import jax.numpy as jnp
from jax import lax
from jax.experimental import pallas as pl
from jax.experimental.pallas import tpu as pltpu
from jax.sharding import PartitionSpec as P

MESH = pl.DeviceIdType.MESH


def factor(count, rows):
    low = 1
    while low * low < count or count % low or rows % low:
        low += 1
    return count // low, low


def shifted(value, width):
    n = value.shape[0]
    column = lax.rem(lax.broadcasted_iota(jnp.int32, value.shape, 0), width)
    left = jnp.where(column == 0, 0.0, pltpu.roll(value, 1, 0))
    right = jnp.where(column == width - 1, 0.0, pltpu.roll(value, n - 1, 0))
    return left, value, right


def kernel(n_tm, n_chan, frames_ref, win_ref, codes_ref, wout_ref, out_ref,
           fpad, spad, loc, recv_a, pre, total, recv_b, carry, part, recv_d, win, wout,
           w_sem, a_send, a_recv, b_send, b_recv, c_send, c_recv, d_send, d_recv):
    frame_count, height, width, cin = frames_ref.shape
    p = win_ref.shape[-1]
    groups = loc.shape[0]
    pg = p // groups
    hi, lo = factor(n_tm, height)
    block = height // lo
    own_rows = height // n_chan
    me = lax.axis_index("tm")
    chan = lax.axis_index("chan")
    high, low = me // lo, lax.rem(me, lo)

    def mate(k):
        return lax.rem(low + k, lo)

    def at_tm(index):
        return {"tm": index, "chan": chan}

    def at_chan(index):
        return {"tm": me, "chan": index}

    load_in = pltpu.make_async_copy(win_ref, win, w_sem.at[0])
    load_out = pltpu.make_async_copy(wout_ref, wout, w_sem.at[1])
    load_in.start()
    load_out.start()

    barrier = pltpu.get_barrier_semaphore()
    for k in range(1, lo):
        pl.semaphore_signal(barrier, inc=1, device_id=at_tm(high * lo + mate(k)), device_id_type=MESH)
    for k in range(1, n_chan):
        pl.semaphore_signal(barrier, inc=1, device_id=at_chan(lax.rem(chan + k, n_chan)), device_id_type=MESH)

    @pl.when(high > 0)
    def _():
        pl.semaphore_signal(barrier, inc=1, device_id=at_tm(me - lo), device_id_type=MESH)

    @pl.when(high < hi - 1)
    def _():
        pl.semaphore_signal(barrier, inc=1, device_id=at_tm(me + lo), device_id_type=MESH)

    fpad[:, 0] = jnp.zeros((frame_count, width, 3 * cin), jnp.bfloat16)
    fpad[:, height + 1] = jnp.zeros((frame_count, width, 3 * cin), jnp.bfloat16)
    spad[:, 0] = jnp.zeros((frame_count, width, p), jnp.bfloat16)
    spad[:, height + 1] = jnp.zeros((frame_count, width, p), jnp.bfloat16)

    @pl.loop(0, frame_count)
    def _(f):
        value = frames_ref[f].astype(jnp.float32).reshape(height * width, cin)
        for dj, piece in enumerate(shifted(value, width)):
            fpad[f, 1 : height + 1, :, dj * cin : (dj + 1) * cin] = piece.astype(jnp.bfloat16).reshape(height, width, cin)

    decay = 1.0 - codes_ref[...].astype(jnp.float32) / 4096.0
    powers = [decay]
    for _ in range(1, frame_count):
        powers.append(powers[-1] * decay)
    step = powers[-1]
    steps = [jnp.ones_like(step)]
    for _ in range(lo):
        steps.append(steps[-1] * step)

    peers = lo + n_chan - 2 + jnp.where(high > 0, 1, 0) + jnp.where(high < hi - 1, 1, 0)
    pl.semaphore_wait(barrier, peers)

    def lanes(vectors, g):
        return [vector[:, g * pg : (g + 1) * pg] for vector in vectors]

    def copy_a(g, k):
        return pltpu.make_async_remote_copy(
            src_ref=loc.at[g, frame_count - 1, pl.ds(mate(k) * block, block)],
            dst_ref=recv_a.at[g, low],
            send_sem=a_send.at[g, k], recv_sem=a_recv.at[g, k],
            device_id=at_tm(high * lo + mate(k)), device_id_type=MESH)

    def copy_b(g, row):
        return pltpu.make_async_remote_copy(
            src_ref=total.at[g, row], dst_ref=recv_b.at[g, row],
            send_sem=b_send.at[g, row], recv_sem=b_recv.at[g, row],
            device_id=at_tm(lax.rem(me + lo, n_tm)), device_id_type=MESH)

    def copy_c(g, k, row):
        return pltpu.make_async_remote_copy(
            src_ref=pre.at[g, mate(k), row], dst_ref=carry.at[g, low * block + row],
            send_sem=c_send.at[g, k, row], recv_sem=c_recv.at[g, k, row],
            device_id=at_tm(high * lo + mate(k)), device_id_type=MESH)

    load_in.wait()
    for g in range(groups):
        (rate,) = lanes([decay], g)
        for k in list(range(1, lo)) + [0]:
            first = mate(k) * block
            taps = [fpad[:, pl.ds(first + di, block)].reshape(frame_count * block * width, 3 * cin) for di in range(3)]
            lhs = jnp.concatenate(taps, axis=1)
            drive = jnp.dot(lhs, win[:, g * pg : (g + 1) * pg], preferred_element_type=jnp.float32)
            drive = drive.reshape(frame_count, block * width, pg)
            running = drive[0]
            loc[g, 0, pl.ds(first, block)] = running.reshape(block, width, pg)
            for f in range(1, frame_count):
                running = rate * running + drive[f]
                loc[g, f, pl.ds(first, block)] = running.reshape(block, width, pg)
            if k:
                copy_a(g, k).start()
            else:
                recv_a[g, low] = running.reshape(block, width, pg)

    for g in range(groups):
        jumps = lanes(steps, g)
        for k in range(1, lo):
            copy_a(g, k).wait_recv()
        for row in range(block):
            running = jnp.zeros((width, pg), jnp.float32)
            for i in range(lo):
                pre[g, i, row] = running
                running = jumps[1] * running + recv_a[g, i, row]
            total[g, row] = running
        for row in range(block):
            @pl.when(high == 0)
            def _():
                recv_b[g, row] = jnp.zeros((width, pg), jnp.float32)

            @pl.when(high > 0)
            def _():
                copy_b(g, row).wait_recv()

            entering = recv_b[g, row]

            @pl.when(high < hi - 1)
            def _():
                total[g, row] = jumps[lo] * entering + total[g, row]
                copy_b(g, row).start()

            for i in range(lo):
                pre[g, i, row] = pre[g, i, row] + jumps[i] * entering
            for k in range(1, lo):
                copy_c(g, k, row).start()
            carry[g, low * block + row] = pre[g, low, row]

    piece_rows = min(own_rows, 4)

    def copy_d(k, start):
        rows = slice(start, start + piece_rows)
        return pltpu.make_async_remote_copy(
            src_ref=part.at[k, :, rows], dst_ref=recv_d.at[k, :, rows],
            send_sem=d_send.at[k, start // piece_rows], recv_sem=d_recv.at[k, start // piece_rows],
            device_id=at_chan(lax.rem(chan + k, n_chan)), device_id_type=MESH)

    load_out.wait()
    for g in range(groups):
        rates = lanes(powers, g)
        for k in range(lo):
            source = lax.rem(low + lo - k, lo)
            if k:
                for row in range(block):
                    copy_c(g, k, row).wait_recv()
            first = source * block
            entering = carry[g, pl.ds(first, block)].reshape(block * width, pg)
            for f in range(frame_count):
                value = loc[g, f, pl.ds(first, block)].reshape(block * width, pg) + rates[f] * entering
                spad[f, pl.ds(first + 1, block), :, g * pg : (g + 1) * pg] = value.astype(jnp.bfloat16).reshape(block, width, pg)
        for k in list(range(1, n_chan)) + [0]:
            for start in range(0, own_rows, piece_rows):
                first = lax.rem(chan + k, n_chan) * own_rows + start
                taps = [spad[:, pl.ds(first + di, piece_rows), :, g * pg : (g + 1) * pg] for di in range(3)]
                lhs = jnp.concatenate([tap.reshape(frame_count * piece_rows * width, pg) for tap in taps], axis=1)
                columns = []
                for dj in range(3):
                    rhs = jnp.concatenate([wout[di, dj, g * pg : (g + 1) * pg] for di in range(3)], axis=0)
                    columns.append(jnp.dot(lhs, rhs, preferred_element_type=jnp.float32))
                readout = columns[1] + shifted(columns[0], width)[0] + shifted(columns[2], width)[2]
                readout = readout.reshape(frame_count, piece_rows, width, cin)
                if g:
                    readout = readout + part[k, :, start : start + piece_rows]
                part[k, :, start : start + piece_rows] = readout
                if k and g == groups - 1:
                    copy_d(k, start).start()

    for start in range(0, own_rows, piece_rows):
        rows = slice(start, start + piece_rows)
        value = part[0, :, rows]
        for k in range(1, n_chan):
            copy_d(k, start).wait_recv()
            value = value + recv_d[k, :, rows]
        out_ref[:, rows] = value

    for k in range(1, n_chan):
        for start in range(0, own_rows, piece_rows):
            copy_d(k, start).wait_send()
    for g in range(groups):
        for k in range(1, lo):
            copy_a(g, k).wait_send()
            for row in range(block):
                copy_c(g, k, row).wait_send()
        for row in range(block):
            @pl.when(high < hi - 1)
            def _():
                copy_b(g, row).wait_send()


def per_device(n_tm, n_chan, frames, in_weight, decay_codes, out_weight, skip_gain):
    frame_count, height, width, cin = frames.shape
    p = in_weight.shape[-1]
    hi, lo = factor(n_tm, height)
    block = height // lo
    own_rows = height // n_chan
    groups = 2 if p % 512 == 0 else 1
    pg = p // groups
    f32, bf16 = jnp.float32, jnp.bfloat16
    dma = pltpu.SemaphoreType.DMA
    summed = pl.pallas_call(
        functools.partial(kernel, n_tm, n_chan),
        out_shape=jax.ShapeDtypeStruct((frame_count, own_rows, width, cin), f32),
        in_specs=[
            pl.BlockSpec(memory_space=pltpu.VMEM),
            pl.BlockSpec(memory_space=pl.ANY),
            pl.BlockSpec(memory_space=pltpu.VMEM),
            pl.BlockSpec(memory_space=pl.ANY),
        ],
        out_specs=pl.BlockSpec(memory_space=pltpu.VMEM),
        scratch_shapes=[
            pltpu.VMEM((frame_count, height + 2, width, 3 * cin), bf16),
            pltpu.VMEM((frame_count, height + 2, width, p), bf16),
            pltpu.VMEM((groups, frame_count, height, width, pg), f32),
            pltpu.VMEM((groups, lo, block, width, pg), f32),
            pltpu.VMEM((groups, lo, block, width, pg), f32),
            pltpu.VMEM((groups, block, width, pg), f32),
            pltpu.VMEM((groups, block, width, pg), f32),
            pltpu.VMEM((groups, height, width, pg), f32),
            pltpu.VMEM((n_chan, frame_count, own_rows, width, cin), f32),
            pltpu.VMEM((n_chan, frame_count, own_rows, width, cin), f32),
            pltpu.VMEM((9 * cin, p), bf16),
            pltpu.VMEM((3, 3, p, cin), bf16),
            dma((2,)), dma((groups, lo)), dma((groups, lo)), dma((groups, block)), dma((groups, block)),
            dma((groups, lo, block)), dma((groups, lo, block)), dma((n_chan, own_rows)), dma((n_chan, own_rows)),
        ],
        compiler_params=pltpu.CompilerParams(
            collective_id=0, has_side_effects=True, vmem_limit_bytes=56 * 1024 * 1024),
    )(
        frames,
        in_weight.reshape(9 * cin, p),
        decay_codes.reshape(1, p),
        out_weight,
    )
    start_row = lax.axis_index("chan") * own_rows
    own_frames = lax.dynamic_slice_in_dim(frames, start_row, own_rows, 1).astype(f32)
    value = summed + skip_gain * own_frames
    return (0.5 * value * (1.0 + lax.erf(value * 0.5**0.5))).astype(bf16)


def solution(mesh):
    return jax.shard_map(
        functools.partial(per_device, mesh.shape["tm"], mesh.shape["chan"]),
        mesh=mesh,
        in_specs=(
            P("tm", None, None, None),
            P(None, None, None, "chan"),
            P("chan"),
            P(None, None, "chan", None),
            P(),
        ),
        out_specs=P("tm", "chan", None, None),
        check_vma=False,
    )
```

```python
import functools

import jax
import jax.numpy as jnp
from jax import lax
from jax.experimental import pallas as pl
from jax.experimental.pallas import tpu as pltpu
from jax.sharding import PartitionSpec as P

MESH = pl.DeviceIdType.MESH


def factor(count, rows):
    low = 1
    while low * low < count or count % low or rows % low:
        low += 1
    return count // low, low


def shifted(value, width):
    n = value.shape[0]
    column = lax.rem(lax.broadcasted_iota(jnp.int32, value.shape, 0), width)
    left = jnp.where(column == 0, 0.0, pltpu.roll(value, 1, 0))
    right = jnp.where(column == width - 1, 0.0, pltpu.roll(value, n - 1, 0))
    return left, value, right


def kernel(n_tm, n_chan, frames_ref, win_ref, codes_ref, wout_ref, out_ref,
           fpad, spad, loc, recv_a, pre, total, recv_b, carry, part, recv_d, win, wout,
           w_sem, a_send, a_recv, b_send, b_recv, c_send, c_recv, d_send, d_recv):
    frame_count, height, width, cin = frames_ref.shape
    p = win_ref.shape[-1]
    groups = loc.shape[0]
    pg = p // groups
    hi, lo = factor(n_tm, height)
    block = height // lo
    own_rows = height // n_chan
    me = lax.axis_index("tm")
    chan = lax.axis_index("chan")
    high, low = me // lo, lax.rem(me, lo)

    def mate(k):
        return lax.rem(low + k, lo)

    def at_tm(index):
        return {"tm": index, "chan": chan}

    def at_chan(index):
        return {"tm": me, "chan": index}

    load_in = pltpu.make_async_copy(win_ref, win, w_sem.at[0])
    load_out = pltpu.make_async_copy(wout_ref, wout, w_sem.at[1])
    load_in.start()
    load_out.start()

    barrier = pltpu.get_barrier_semaphore()
    for k in range(1, lo):
        pl.semaphore_signal(barrier, inc=1, device_id=at_tm(high * lo + mate(k)), device_id_type=MESH)
    for k in range(1, n_chan):
        pl.semaphore_signal(barrier, inc=1, device_id=at_chan(lax.rem(chan + k, n_chan)), device_id_type=MESH)

    @pl.when(high > 0)
    def _():
        pl.semaphore_signal(barrier, inc=1, device_id=at_tm(me - lo), device_id_type=MESH)

    @pl.when(high < hi - 1)
    def _():
        pl.semaphore_signal(barrier, inc=1, device_id=at_tm(me + lo), device_id_type=MESH)

    fpad[:, 0] = jnp.zeros((frame_count, width, 3 * cin), jnp.bfloat16)
    fpad[:, height + 1] = jnp.zeros((frame_count, width, 3 * cin), jnp.bfloat16)
    spad[:, 0] = jnp.zeros((frame_count, width, p), jnp.bfloat16)
    spad[:, height + 1] = jnp.zeros((frame_count, width, p), jnp.bfloat16)

    @pl.loop(0, frame_count)
    def _(f):
        value = frames_ref[f].astype(jnp.float32).reshape(height * width, cin)
        for dj, piece in enumerate(shifted(value, width)):
            fpad[f, 1 : height + 1, :, dj * cin : (dj + 1) * cin] = piece.astype(jnp.bfloat16).reshape(height, width, cin)

    decay = 1.0 - codes_ref[...].astype(jnp.float32) / 4096.0
    powers = [decay]
    for _ in range(1, frame_count):
        powers.append(powers[-1] * decay)
    step = powers[-1]
    steps = [jnp.ones_like(step)]
    for _ in range(lo):
        steps.append(steps[-1] * step)

    peers = lo + n_chan - 2 + jnp.where(high > 0, 1, 0) + jnp.where(high < hi - 1, 1, 0)

    def lanes(vectors, g):
        return [vector[:, g * pg : (g + 1) * pg] for vector in vectors]

    def copy_a(g, k):
        return pltpu.make_async_remote_copy(
            src_ref=loc.at[g, frame_count - 1, pl.ds(mate(k) * block, block)],
            dst_ref=recv_a.at[g, low],
            send_sem=a_send.at[g, k], recv_sem=a_recv.at[g, k],
            device_id=at_tm(high * lo + mate(k)), device_id_type=MESH)

    def copy_b(g, row):
        return pltpu.make_async_remote_copy(
            src_ref=total.at[g, row], dst_ref=recv_b.at[g, row],
            send_sem=b_send.at[g, row], recv_sem=b_recv.at[g, row],
            device_id=at_tm(lax.rem(me + lo, n_tm)), device_id_type=MESH)

    def copy_c(g, k, row):
        return pltpu.make_async_remote_copy(
            src_ref=pre.at[g, mate(k), row], dst_ref=carry.at[g, low * block + row],
            send_sem=c_send.at[g, k, row], recv_sem=c_recv.at[g, k, row],
            device_id=at_tm(high * lo + mate(k)), device_id_type=MESH)

    first_mate = 1 if lo > 1 else 0
    load_in.wait()
    for g in range(groups):
        (rate,) = lanes([decay], g)
        for k in list(range(1, lo)) + [0]:
            first = mate(k) * block
            taps = [fpad[:, pl.ds(first + di, block)].reshape(frame_count * block * width, 3 * cin) for di in range(3)]
            lhs = jnp.concatenate(taps, axis=1)
            drive = jnp.dot(lhs, win[:, g * pg : (g + 1) * pg], preferred_element_type=jnp.float32)
            drive = drive.reshape(frame_count, block * width, pg)
            running = drive[0]
            loc[g, 0, pl.ds(first, block)] = running.reshape(block, width, pg)
            for f in range(1, frame_count):
                running = rate * running + drive[f]
                loc[g, f, pl.ds(first, block)] = running.reshape(block, width, pg)
            if g == 0 and k == first_mate:
                pl.semaphore_wait(barrier, peers)
            if k:
                copy_a(g, k).start()
            else:
                recv_a[g, low] = running.reshape(block, width, pg)

    for g in range(groups):
        jumps = lanes(steps, g)
        for k in range(1, lo):
            copy_a(g, k).wait_recv()
        for row in range(block):
            running = recv_a[g, 0, row]
            for i in range(1, lo):
                running = jumps[1] * running + recv_a[g, i, row]
            total[g, row] = running
        for row in range(block):
            @pl.when(high == 0)
            def _():
                recv_b[g, row] = jnp.zeros((width, pg), jnp.float32)

            @pl.when(high > 0)
            def _():
                copy_b(g, row).wait_recv()

            @pl.when(high < hi - 1)
            def _():
                total[g, row] = jumps[lo] * recv_b[g, row] + total[g, row]
                copy_b(g, row).start()

        for row in range(block):
            running = recv_b[g, row]
            for i in range(lo):
                pre[g, i, row] = running
                running = jumps[1] * running + recv_a[g, i, row]
            for k in range(1, lo):
                copy_c(g, k, row).start()
            carry[g, low * block + row] = pre[g, low, row]

    piece_rows = min(own_rows, 4)

    def copy_d(k, start):
        rows = slice(start, start + piece_rows)
        return pltpu.make_async_remote_copy(
            src_ref=part.at[k, :, rows], dst_ref=recv_d.at[k, :, rows],
            send_sem=d_send.at[k, start // piece_rows], recv_sem=d_recv.at[k, start // piece_rows],
            device_id=at_chan(lax.rem(chan + k, n_chan)), device_id_type=MESH)

    load_out.wait()
    for g in range(groups):
        rates = lanes(powers, g)
        for k in range(lo):
            source = lax.rem(low + lo - k, lo)
            if k:
                for row in range(block):
                    copy_c(g, k, row).wait_recv()
            first = source * block
            entering = carry[g, pl.ds(first, block)].reshape(block * width, pg)
            for f in range(frame_count):
                value = loc[g, f, pl.ds(first, block)].reshape(block * width, pg) + rates[f] * entering
                spad[f, pl.ds(first + 1, block), :, g * pg : (g + 1) * pg] = value.astype(jnp.bfloat16).reshape(block, width, pg)
        for k in list(range(1, n_chan)) + [0]:
            for start in range(0, own_rows, piece_rows):
                first = lax.rem(chan + k, n_chan) * own_rows + start
                taps = [spad[:, pl.ds(first + di, piece_rows), :, g * pg : (g + 1) * pg] for di in range(3)]
                lhs = jnp.concatenate([tap.reshape(frame_count * piece_rows * width, pg) for tap in taps], axis=1)
                columns = []
                for dj in range(3):
                    rhs = jnp.concatenate([wout[di, dj, g * pg : (g + 1) * pg] for di in range(3)], axis=0)
                    columns.append(jnp.dot(lhs, rhs, preferred_element_type=jnp.float32))
                readout = columns[1] + shifted(columns[0], width)[0] + shifted(columns[2], width)[2]
                readout = readout.reshape(frame_count, piece_rows, width, cin)
                if g:
                    readout = readout + part[k, :, start : start + piece_rows]
                part[k, :, start : start + piece_rows] = readout
                if k and g == groups - 1:
                    copy_d(k, start).start()

    for start in range(0, own_rows, piece_rows):
        rows = slice(start, start + piece_rows)
        value = part[0, :, rows]
        for k in range(1, n_chan):
            copy_d(k, start).wait_recv()
            value = value + recv_d[k, :, rows]
        out_ref[:, rows] = value

    for k in range(1, n_chan):
        for start in range(0, own_rows, piece_rows):
            copy_d(k, start).wait_send()
    for g in range(groups):
        for k in range(1, lo):
            copy_a(g, k).wait_send()
            for row in range(block):
                copy_c(g, k, row).wait_send()
        for row in range(block):
            @pl.when(high < hi - 1)
            def _():
                copy_b(g, row).wait_send()


def per_device(n_tm, n_chan, frames, in_weight, decay_codes, out_weight, skip_gain):
    frame_count, height, width, cin = frames.shape
    p = in_weight.shape[-1]
    hi, lo = factor(n_tm, height)
    block = height // lo
    own_rows = height // n_chan
    groups = 2 if p % 512 == 0 else 1
    pg = p // groups
    f32, bf16 = jnp.float32, jnp.bfloat16
    dma = pltpu.SemaphoreType.DMA
    summed = pl.pallas_call(
        functools.partial(kernel, n_tm, n_chan),
        out_shape=jax.ShapeDtypeStruct((frame_count, own_rows, width, cin), f32),
        in_specs=[
            pl.BlockSpec(memory_space=pltpu.VMEM),
            pl.BlockSpec(memory_space=pl.ANY),
            pl.BlockSpec(memory_space=pltpu.VMEM),
            pl.BlockSpec(memory_space=pl.ANY),
        ],
        out_specs=pl.BlockSpec(memory_space=pltpu.VMEM),
        scratch_shapes=[
            pltpu.VMEM((frame_count, height + 2, width, 3 * cin), bf16),
            pltpu.VMEM((frame_count, height + 2, width, p), bf16),
            pltpu.VMEM((groups, frame_count, height, width, pg), f32),
            pltpu.VMEM((groups, lo, block, width, pg), f32),
            pltpu.VMEM((groups, lo, block, width, pg), f32),
            pltpu.VMEM((groups, block, width, pg), f32),
            pltpu.VMEM((groups, block, width, pg), f32),
            pltpu.VMEM((groups, height, width, pg), f32),
            pltpu.VMEM((n_chan, frame_count, own_rows, width, cin), f32),
            pltpu.VMEM((n_chan, frame_count, own_rows, width, cin), f32),
            pltpu.VMEM((9 * cin, p), bf16),
            pltpu.VMEM((3, 3, p, cin), bf16),
            dma((2,)), dma((groups, lo)), dma((groups, lo)), dma((groups, block)), dma((groups, block)),
            dma((groups, lo, block)), dma((groups, lo, block)), dma((n_chan, own_rows)), dma((n_chan, own_rows)),
        ],
        compiler_params=pltpu.CompilerParams(
            collective_id=0, has_side_effects=True, vmem_limit_bytes=56 * 1024 * 1024),
    )(
        frames,
        in_weight.reshape(9 * cin, p),
        decay_codes.reshape(1, p),
        out_weight,
    )
    start_row = lax.axis_index("chan") * own_rows
    own_frames = lax.dynamic_slice_in_dim(frames, start_row, own_rows, 1).astype(f32)
    value = summed + skip_gain * own_frames
    return (0.5 * value * (1.0 + lax.erf(value * 0.5**0.5))).astype(bf16)


def solution(mesh):
    return jax.shard_map(
        functools.partial(per_device, mesh.shape["tm"], mesh.shape["chan"]),
        mesh=mesh,
        in_specs=(
            P("tm", None, None, None),
            P(None, None, None, "chan"),
            P("chan"),
            P(None, None, "chan", None),
            P(),
        ),
        out_specs=P("tm", "chan", None, None),
        check_vma=False,
    )
```

```python
import functools

import jax
import jax.numpy as jnp
from jax import lax
from jax.experimental import pallas as pl
from jax.experimental.pallas import tpu as pltpu
from jax.sharding import PartitionSpec as P

MESH = pl.DeviceIdType.MESH


def factor(count, rows):
    low = 1
    while low * low < count or count % low or rows % low:
        low += 1
    return count // low, low


def shifted(value, width):
    n = value.shape[0]
    column = lax.rem(lax.broadcasted_iota(jnp.int32, value.shape, 0), width)
    left = jnp.where(column == 0, 0.0, pltpu.roll(value, 1, 0))
    right = jnp.where(column == width - 1, 0.0, pltpu.roll(value, n - 1, 0))
    return left, value, right


def kernel(n_tm, n_chan, frames_ref, win_ref, codes_ref, wout_ref, skip_ref, out_ref,
           fpad, spad, loc, recv_a, pre, total, recv_b, carry, part, recv_d, win, wout,
           w_sem, a_send, a_recv, b_send, b_recv, c_send, c_recv, d_send, d_recv):
    frame_count, height, width, cin = frames_ref.shape
    p = win_ref.shape[-1]
    groups = loc.shape[0]
    pg = p // groups
    hi, lo = factor(n_tm, height)
    block = height // lo
    own_rows = height // n_chan
    me = lax.axis_index("tm")
    chan = lax.axis_index("chan")
    high, low = me // lo, lax.rem(me, lo)

    def mate(k):
        return lax.rem(low + k, lo)

    def at_tm(index):
        return {"tm": index, "chan": chan}

    def at_chan(index):
        return {"tm": me, "chan": index}

    load_in = pltpu.make_async_copy(win_ref, win, w_sem.at[0])
    load_out = pltpu.make_async_copy(wout_ref, wout, w_sem.at[1])
    load_in.start()
    load_out.start()

    barrier = pltpu.get_barrier_semaphore()
    for k in range(1, lo):
        pl.semaphore_signal(barrier, inc=1, device_id=at_tm(high * lo + mate(k)), device_id_type=MESH)
    for k in range(1, n_chan):
        pl.semaphore_signal(barrier, inc=1, device_id=at_chan(lax.rem(chan + k, n_chan)), device_id_type=MESH)

    @pl.when(high > 0)
    def _():
        pl.semaphore_signal(barrier, inc=1, device_id=at_tm(me - lo), device_id_type=MESH)

    @pl.when(high < hi - 1)
    def _():
        pl.semaphore_signal(barrier, inc=1, device_id=at_tm(me + lo), device_id_type=MESH)

    fpad[:, 0] = jnp.zeros((frame_count, width, 3 * cin), jnp.bfloat16)
    fpad[:, height + 1] = jnp.zeros((frame_count, width, 3 * cin), jnp.bfloat16)
    spad[:, 0] = jnp.zeros((frame_count, width, p), jnp.bfloat16)
    spad[:, height + 1] = jnp.zeros((frame_count, width, p), jnp.bfloat16)

    @pl.loop(0, frame_count)
    def _(f):
        value = frames_ref[f].astype(jnp.float32).reshape(height * width, cin)
        for dj, piece in enumerate(shifted(value, width)):
            fpad[f, 1 : height + 1, :, dj * cin : (dj + 1) * cin] = piece.astype(jnp.bfloat16).reshape(height, width, cin)

    decay = 1.0 - codes_ref[...].astype(jnp.float32) / 4096.0
    powers = [decay]
    for _ in range(1, frame_count):
        powers.append(powers[-1] * decay)
    step = powers[-1]
    steps = [jnp.ones_like(step)]
    for _ in range(lo):
        steps.append(steps[-1] * step)

    peers = lo + n_chan - 2 + jnp.where(high > 0, 1, 0) + jnp.where(high < hi - 1, 1, 0)
    pl.semaphore_wait(barrier, peers)

    def lanes(vectors, g):
        return [vector[:, g * pg : (g + 1) * pg] for vector in vectors]

    def copy_a(g, k):
        return pltpu.make_async_remote_copy(
            src_ref=loc.at[g, frame_count - 1, pl.ds(mate(k) * block, block)],
            dst_ref=recv_a.at[g, low],
            send_sem=a_send.at[g, k], recv_sem=a_recv.at[g, k],
            device_id=at_tm(high * lo + mate(k)), device_id_type=MESH)

    def copy_b(g, row):
        return pltpu.make_async_remote_copy(
            src_ref=total.at[g, row], dst_ref=recv_b.at[g, row],
            send_sem=b_send.at[g, row], recv_sem=b_recv.at[g, row],
            device_id=at_tm(lax.rem(me + lo, n_tm)), device_id_type=MESH)

    def copy_c(g, k, row):
        return pltpu.make_async_remote_copy(
            src_ref=pre.at[g, mate(k), row], dst_ref=carry.at[g, low * block + row],
            send_sem=c_send.at[g, k, row], recv_sem=c_recv.at[g, k, row],
            device_id=at_tm(high * lo + mate(k)), device_id_type=MESH)

    load_in.wait()
    for g in range(groups):
        (rate,) = lanes([decay], g)
        for k in list(range(1, lo)) + [0]:
            first = mate(k) * block
            taps = [fpad[:, pl.ds(first + di, block)].reshape(frame_count * block * width, 3 * cin) for di in range(3)]
            lhs = jnp.concatenate(taps, axis=1)
            drive = jnp.dot(lhs, win[:, g * pg : (g + 1) * pg], preferred_element_type=jnp.float32)
            drive = drive.reshape(frame_count, block * width, pg)
            running = drive[0]
            loc[g, 0, pl.ds(first, block)] = running.reshape(block, width, pg)
            for f in range(1, frame_count):
                running = rate * running + drive[f]
                loc[g, f, pl.ds(first, block)] = running.reshape(block, width, pg)
            if k:
                copy_a(g, k).start()
            else:
                recv_a[g, low] = running.reshape(block, width, pg)

    for g in range(groups):
        jumps = lanes(steps, g)
        for k in range(1, lo):
            copy_a(g, k).wait_recv()
        for row in range(block):
            running = jnp.zeros((width, pg), jnp.float32)
            for i in range(lo):
                pre[g, i, row] = running
                running = jumps[1] * running + recv_a[g, i, row]
            total[g, row] = running
        for row in range(block):
            @pl.when(high == 0)
            def _():
                recv_b[g, row] = jnp.zeros((width, pg), jnp.float32)

            @pl.when(high > 0)
            def _():
                copy_b(g, row).wait_recv()

            entering = recv_b[g, row]

            @pl.when(high < hi - 1)
            def _():
                total[g, row] = jumps[lo] * entering + total[g, row]
                copy_b(g, row).start()

            for i in range(lo):
                pre[g, i, row] = pre[g, i, row] + jumps[i] * entering
            for k in range(1, lo):
                copy_c(g, k, row).start()
            carry[g, low * block + row] = pre[g, low, row]

    piece_rows = min(own_rows, 4)

    def copy_d(k, start):
        rows = slice(start, start + piece_rows)
        return pltpu.make_async_remote_copy(
            src_ref=part.at[k, :, rows], dst_ref=recv_d.at[k, :, rows],
            send_sem=d_send.at[k, start // piece_rows], recv_sem=d_recv.at[k, start // piece_rows],
            device_id=at_chan(lax.rem(chan + k, n_chan)), device_id_type=MESH)

    load_out.wait()
    for g in range(groups):
        rates = lanes(powers, g)
        for k in range(lo):
            source = lax.rem(low + lo - k, lo)
            if k:
                for row in range(block):
                    copy_c(g, k, row).wait_recv()
            first = source * block
            entering = carry[g, pl.ds(first, block)].reshape(block * width, pg)
            for f in range(frame_count):
                value = loc[g, f, pl.ds(first, block)].reshape(block * width, pg) + rates[f] * entering
                spad[f, pl.ds(first + 1, block), :, g * pg : (g + 1) * pg] = value.astype(jnp.bfloat16).reshape(block, width, pg)
        for k in list(range(1, n_chan)) + [0]:
            for start in range(0, own_rows, piece_rows):
                first = lax.rem(chan + k, n_chan) * own_rows + start
                taps = [spad[:, pl.ds(first + di, piece_rows), :, g * pg : (g + 1) * pg] for di in range(3)]
                lhs = jnp.concatenate([tap.reshape(frame_count * piece_rows * width, pg) for tap in taps], axis=1)
                columns = []
                for dj in range(3):
                    rhs = jnp.concatenate([wout[di, dj, g * pg : (g + 1) * pg] for di in range(3)], axis=0)
                    columns.append(jnp.dot(lhs, rhs, preferred_element_type=jnp.float32))
                readout = columns[1] + shifted(columns[0], width)[0] + shifted(columns[2], width)[2]
                readout = readout.reshape(frame_count, piece_rows, width, cin)
                if g:
                    readout = readout + part[k, :, start : start + piece_rows]
                part[k, :, start : start + piece_rows] = readout
                if k and g == groups - 1:
                    copy_d(k, start).start()

    for start in range(0, own_rows, piece_rows):
        rows = slice(start, start + piece_rows)
        value = part[0, :, rows]
        for k in range(1, n_chan):
            copy_d(k, start).wait_recv()
            value = value + recv_d[k, :, rows]
        own = frames_ref[:, pl.ds(chan * own_rows + start, piece_rows)].astype(jnp.float32)
        value = value + skip_ref[...].reshape(1, 1, 1, cin) * own
        out_ref[:, rows] = (0.5 * value * (1.0 + lax.erf(value * 0.5**0.5))).astype(jnp.bfloat16)

    for k in range(1, n_chan):
        for start in range(0, own_rows, piece_rows):
            copy_d(k, start).wait_send()
    for g in range(groups):
        for k in range(1, lo):
            copy_a(g, k).wait_send()
            for row in range(block):
                copy_c(g, k, row).wait_send()
        for row in range(block):
            @pl.when(high < hi - 1)
            def _():
                copy_b(g, row).wait_send()


def per_device(n_tm, n_chan, frames, in_weight, decay_codes, out_weight, skip_gain):
    frame_count, height, width, cin = frames.shape
    p = in_weight.shape[-1]
    hi, lo = factor(n_tm, height)
    block = height // lo
    own_rows = height // n_chan
    groups = 2 if p % 512 == 0 else 1
    pg = p // groups
    f32, bf16 = jnp.float32, jnp.bfloat16
    dma = pltpu.SemaphoreType.DMA
    summed = pl.pallas_call(
        functools.partial(kernel, n_tm, n_chan),
        out_shape=jax.ShapeDtypeStruct((frame_count, own_rows, width, cin), bf16),
        in_specs=[
            pl.BlockSpec(memory_space=pltpu.VMEM),
            pl.BlockSpec(memory_space=pl.ANY),
            pl.BlockSpec(memory_space=pltpu.VMEM),
            pl.BlockSpec(memory_space=pl.ANY),
            pl.BlockSpec(memory_space=pltpu.VMEM),
        ],
        out_specs=pl.BlockSpec(memory_space=pltpu.VMEM),
        scratch_shapes=[
            pltpu.VMEM((frame_count, height + 2, width, 3 * cin), bf16),
            pltpu.VMEM((frame_count, height + 2, width, p), bf16),
            pltpu.VMEM((groups, frame_count, height, width, pg), f32),
            pltpu.VMEM((groups, lo, block, width, pg), f32),
            pltpu.VMEM((groups, lo, block, width, pg), f32),
            pltpu.VMEM((groups, block, width, pg), f32),
            pltpu.VMEM((groups, block, width, pg), f32),
            pltpu.VMEM((groups, height, width, pg), f32),
            pltpu.VMEM((n_chan, frame_count, own_rows, width, cin), f32),
            pltpu.VMEM((n_chan, frame_count, own_rows, width, cin), f32),
            pltpu.VMEM((9 * cin, p), bf16),
            pltpu.VMEM((3, 3, p, cin), bf16),
            dma((2,)), dma((groups, lo)), dma((groups, lo)), dma((groups, block)), dma((groups, block)),
            dma((groups, lo, block)), dma((groups, lo, block)), dma((n_chan, own_rows)), dma((n_chan, own_rows)),
        ],
        compiler_params=pltpu.CompilerParams(
            collective_id=0, has_side_effects=True, vmem_limit_bytes=56 * 1024 * 1024),
    )(
        frames,
        in_weight.reshape(9 * cin, p),
        decay_codes.reshape(1, p),
        out_weight,
        skip_gain.reshape(1, cin),
    )
    return summed


def solution(mesh):
    return jax.shard_map(
        functools.partial(per_device, mesh.shape["tm"], mesh.shape["chan"]),
        mesh=mesh,
        in_specs=(
            P("tm", None, None, None),
            P(None, None, None, "chan"),
            P("chan"),
            P(None, None, "chan", None),
            P(),
        ),
        out_specs=P("tm", "chan", None, None),
        check_vma=False,
    )
```
